32 devices in a mesh: group: 2 (over x), chan: 16 (over z, y, core).
Axes of the slice: x: 2, y: 2, z: 4, core: 2. Of those that a mesh axis runs over, the one named last changes fastest.
Arguments:
- parent_state: float32 [32, 16, 16384], P('group', None, 'chan'), parts along dimension 0, may hold values from -6 to 6
- parent_conv: bfloat16 [32, 3, 16384], P('group', None, 'chan'), parts along dimension 0, may hold values from -6 to 6
- fork_map: int32 [32], P('group'), parts along dimension 0, may hold values from 0 to 15
- judge_lengths: int32 [32], P('group'), parts along dimension 0, may hold values from 1 to 16, 128 in all
- mixer_input: bfloat16 [32, 20, 16384], P('group', None, 'chan'), parts along dimension 0, may hold values from -6 to 6
- gate_input: bfloat16 [32, 20, 16384], P('group', None, 'chan'), parts along dimension 0, may hold values from -6 to 6
- conv_weight: bfloat16 [4, 16384], P(None, 'chan'), may hold values from -3 to 3
- conv_bias: float32 [16384], P('chan'), may hold values from -0.5 to 0.5
- rate_down: bfloat16 [16384, 512], P('chan'), may hold values from -0.046875 to 0.046875
- selection_weight: bfloat16 [16384, 32], P('chan'), may hold values from -0.046875 to 0.046875
- rate_up: bfloat16 [512, 16384], P(None, 'chan'), may hold values from -0.25 to 0.25
- rate_bias: float32 [16384], P('chan'), may hold values from -7 to -2.3
- decay_log: float32 [16, 16384], P(None, 'chan'), may hold values from 0 to 2.77
- skip_gain: float32 [16384], P('chan'), may hold values from 0.5 to 1.5
Outputs:
- mixer_output: bfloat16 [32, 20, 16384], P(('group', 'chan')), parts along dimension 0
- final_state: float32 [32, 16, 16384], P(('group', 'chan')), parts along dimension 0
The draws below stay inside these ranges and needn't reach their ends.
There are 2 independent parts, one for each index of `group`. The reference program is written for one: setup_inputs(seed, part) draws one part's arguments, and reference() takes and returns one part's arrays. A program takes and returns all parts, laid end to end along the dimension named above; an argument that names none is the same for every part. Nothing has to cross between parts.
Inputs may be any that keep to these rules, and one draw needn't show every extreme that they name: `fork_map`: index of the parent node a thought continues. `judge_lengths`: the lengths of one part sum to 128 and the longest is exactly 16.
All inputs are finite; a program needn't handle non-finite values.
Results may differ from the reference program's by a relative error of at most 0.0095.
Values may be sent and summed in bfloat16 or wider, within the bound.
A program may use at most 128 MiB of HBM per device.

```python
import math
import jax
import jax.numpy as jnp
import numpy as np
from jax import lax

E = 16384
S = 16
R = 512
CONV = 4
PARENTS = 16
GEN = 4
JUDGE = 16
THOUGHTS = 16
TOK = 20


def touch_ends(values, key, low, top_value):
    longest = values.shape.index(max(values.shape))
    spots = []
    for shift in (0, 1):
        where = [jax.random.randint(jax.random.fold_in(key, axis), (), 0, length) for axis, length in enumerate(values.shape)]
        where[longest] = (where[longest] + shift) % values.shape[longest]
        spots.append(tuple(where))
    return values.at[spots[0]].set(low).at[spots[1]].set(top_value)


def shard_levels(rng, extent, cuts, least, largest):
    loudness, own = 1.0, jax.random.fold_in(rng, 6)
    for dim, parts in cuts:
        heights = jnp.exp(jax.random.uniform(jax.random.fold_in(own, dim), (parts,), jnp.float32, least / len(cuts), largest / len(cuts)))
        loudness = loudness * jnp.repeat(heights, extent[dim] // parts).reshape([-1 if axis == dim else 1 for axis in range(len(extent))])
    return loudness


def rank_table(count, lean):
    portions = [(1 << 20) // math.isqrt(grade ** lean) + 1 for grade in range(1, count + 1)]
    spread = 1 + sum(portions) // (1 << 30)
    return np.cumsum(np.array([max(1, weight // spread) for weight in portions]))


def skewed_ids(key, dims, number_of, slope):
    table = rank_table(number_of, slope)
    pick = jax.random.randint(jax.random.fold_in(key, 1), dims, 0, int(table[number_of - 1]))
    grade = jnp.searchsorted(jnp.asarray(table, jnp.int32), pick, side="right")
    return jax.random.permutation(jax.random.fold_in(key, 2), number_of)[grade].astype(jnp.int32)


def profile(amount, total, most, skew):
    loads = [(1 << 20) // math.isqrt(grade ** skew) + 1 for grade in range(2, amount + 1)]
    spare, counts = total - most - (amount - 1), [1] * (amount - 1)
    while spare > 0:
        candidates = [i for i in range(amount - 1) if counts[i] < most]
        pool, left = sum([loads[i] for i in candidates]), spare
        for i in candidates:
            more = min(most - counts[i], max(1, left * loads[i] // pool), spare)
            counts[i] = counts[i] + more
            spare = spare - more
    return np.array([most] + counts)


def uneven_parts(rng, number_of, total, reach, skew):
    if number_of == 2:
        one = jax.random.randint(rng, (), max(1, total - reach), min(reach, total - 1) + 1)
        return jnp.stack([one, total - one])
    lengths = jnp.asarray(profile(number_of, total, reach, skew), jnp.int32)
    couples = (number_of - 1) // 2
    giver, receiver = lengths[1:1 + 2 * couples:2], lengths[2:2 + 2 * couples:2]
    slack = jnp.minimum(giver - 1, reach - receiver)
    passed = jax.random.randint(jax.random.fold_in(rng, 1), (couples,), 0, 1 << 20) % (slack + 1)
    lengths = lengths.at[1:1 + 2 * couples:2].set(giver - passed).at[2:2 + 2 * couples:2].set(receiver + passed)
    return lengths[jax.random.permutation(jax.random.fold_in(rng, 2), number_of)]


def normal_values(key, dims, deviation, bound, split=(), kind=jnp.bfloat16):
    entries = deviation * jax.random.normal(key, dims, jnp.float32)
    if split:
        entries = entries * shard_levels(key, dims, split, -0.22, 0.18)
    return jnp.clip(entries, -bound, bound).astype(kind)


def setup_inputs(seed: int = 0, part: int = 0) -> dict:
    key_of = jax.random.split(jax.random.key(seed), 15)
    part_splits = jax.random.split(jax.random.fold_in(key_of[14], part), 15)
    return {
        "parent_state": normal_values(part_splits[0], (PARENTS, S, E), 1.0, 6.0, ((2, 16),), jnp.float32),
        "parent_conv": normal_values(part_splits[1], (PARENTS, CONV - 1, E), 1.0, 6.0, ((2, 16),)),
        "fork_map": touch_ends(skewed_ids(part_splits[2], (THOUGHTS,), PARENTS, 2), jax.random.fold_in(part_splits[2], 3), 0, PARENTS - 1).astype(jnp.int32),
        "judge_lengths": uneven_parts(part_splits[3], THOUGHTS, THOUGHTS * JUDGE // 2, JUDGE, 2).astype(jnp.int32),
        "mixer_input": normal_values(part_splits[4], (THOUGHTS, TOK, E), 1.0, 6.0, ((2, 16),)),
        "gate_input": normal_values(part_splits[5], (THOUGHTS, TOK, E), 1.0, 6.0, ((2, 16),)),
        "conv_weight": normal_values(key_of[6], (CONV, E), CONV ** -0.5, 3.0, ((1, 16),)),
        "conv_bias": jnp.clip(jax.random.uniform(key_of[7], (E,), jnp.float32, -0.5, 0.5) * shard_levels(key_of[7], (E,), ((0, 16),), -0.4, 0.0), -0.5, 0.5),
        "rate_down": normal_values(key_of[8], (E, R), E ** -0.5, 0.046875, ((0, 16),)),
        "selection_weight": normal_values(key_of[9], (E, 2 * S), E ** -0.5, 0.046875, ((0, 16),)),
        "rate_up": normal_values(key_of[10], (R, E), R ** -0.5, 0.25, ((1, 16),)),
        "rate_bias": jnp.clip(-7.0 + 4.7 * jax.random.uniform(key_of[11], (E,), jnp.float32) ** shard_levels(key_of[11], (E,), ((0, 16),), -0.2, 0.2), -7.0, -2.3),
        "decay_log": jnp.clip(2.77 * jax.random.uniform(key_of[12], (S, E), jnp.float32) ** shard_levels(key_of[12], (S, E), ((1, 16),), -0.2, 0.2), 0.0, 2.77),
        "skip_gain": jnp.clip(0.5 + 1.0 * jax.random.uniform(key_of[13], (E,), jnp.float32) ** shard_levels(key_of[13], (E,), ((0, 16),), -0.2, 0.2), 0.5, 1.5),
    }


def reference(parent_state, parent_conv, fork_map, judge_lengths, mixer_input, gate_input, conv_weight, conv_bias, rate_down, selection_weight, rate_up, rate_bias, decay_log, skip_gain):
    thought_count, positions, width_all = mixer_input.shape
    start_conv = jnp.take(parent_conv, fork_map, axis=0)
    padded = jnp.concatenate([start_conv, mixer_input], axis=1).astype(jnp.float32)
    tap_weights = conv_weight.astype(jnp.float32)
    summed = conv_bias[None, None, :] + tap_weights[0][None, None, :] * padded[:, 0:positions, :]
    for offset in range(1, CONV):
        summed = summed + tap_weights[offset][None, None, :] * padded[:, offset:offset + positions, :]
    driven = jax.nn.silu(summed).astype(jnp.bfloat16)
    token_rows = driven.reshape(thought_count * positions, width_all)
    rate_low = jnp.dot(token_rows, rate_down, preferred_element_type=jnp.float32).astype(jnp.bfloat16)
    selection = jnp.dot(token_rows, selection_weight, preferred_element_type=jnp.float32)
    step_rate = jax.nn.softplus(jnp.dot(rate_low, rate_up, preferred_element_type=jnp.float32) + rate_bias[None, :])
    position = lax.broadcasted_iota(jnp.int32, (thought_count, positions), 1)
    live_mask = position < (GEN + judge_lengths)[:, None]
    step_rate = step_rate.reshape(thought_count, positions, width_all) * live_mask[:, :, None].astype(jnp.float32)
    selection = selection.reshape(thought_count, positions, 2 * S)
    decay_rate = -jnp.exp(decay_log)
    start_state = jnp.take(parent_state, fork_map, axis=0)

    def advance(carried, pieces):
        drive_rows, gate_rows, rate_rows, select_rows, alive_rows = pieces
        inflow = drive_rows.astype(jnp.float32)
        factor = jnp.exp(rate_rows[:, None, :] * decay_rate[None, :, :])
        push_term = (rate_rows * inflow)[:, None, :] * select_rows[:, :S, None]
        carried = factor * carried + push_term
        readout = jnp.sum(select_rows[:, S:, None] * carried, axis=1)
        result = (readout + skip_gain[None, :] * inflow) * jax.nn.silu(gate_rows.astype(jnp.float32))
        result = jnp.where(alive_rows[:, None], result, 0.0).astype(jnp.bfloat16)
        return carried, result

    final_state, outputs = lax.scan(advance, start_state, (jnp.swapaxes(driven, 0, 1), jnp.swapaxes(gate_input, 0, 1), jnp.swapaxes(step_rate, 0, 1), jnp.swapaxes(selection, 0, 1), jnp.swapaxes(live_mask, 0, 1)))
    return jnp.swapaxes(outputs, 0, 1), final_state
```

```python
import functools
import math

import jax
import jax.numpy as jnp
from jax import lax
from jax.experimental import pallas as pl
from jax.experimental.pallas import tpu as pltpu
from jax.sharding import PartitionSpec as P

GEN = 4
JUDGE = 16
LANES = 128
MESH = pl.DeviceIdType.MESH
F32 = jnp.float32
BF16 = jnp.bfloat16
VMEM_LIMIT = 56 * 1024 * 1024


def live_rank(lengths, thoughts, shape, axis):
    row = lax.broadcasted_iota(jnp.int32, shape, axis)
    thought = jnp.bitwise_and(row, thoughts - 1)
    position = jnp.right_shift(row, int(math.log2(thoughts)))

    def one(t, carried):
        rank, start = carried
        alive = GEN + lengths[t]
        hit = (thought == t) & (position < alive)
        return jnp.where(hit, start + position, rank), start + alive

    return lax.fori_loop(0, thoughts, one, (jnp.full(shape, -1, jnp.int32), jnp.int32(0)))[0]


def project_kernel(
    fork, lengths, x_ref, start_ref, taps_ref, bias_ref, down_ref, select_ref,
    part_ref, drive_ref, window, drive16,
):
    thoughts, positions, width = x_ref.shape
    tiles, rows = width // LANES, thoughts * positions
    conv = taps_ref.shape[0]
    live = thoughts * (GEN + JUDGE // 2)

    def fill(t, _):
        begin = start_ref[fork[t]].astype(F32)
        fresh = x_ref[t].astype(F32)
        for j in range(tiles):
            lane = slice(j * LANES, (j + 1) * LANES)
            window[j, pl.ds(t, conv - 1, stride=thoughts), :] = begin[:, lane]
            window[j, pl.ds((conv - 1) * thoughts + t, positions, stride=thoughts), :] = fresh[:, lane]
        return 0

    lax.fori_loop(0, thoughts, fill, 0)
    taps = taps_ref[...].astype(F32)

    def convolve(p, _):
        base = pl.multiple_of(p * thoughts, thoughts)
        for j in range(tiles):
            lane = slice(j * LANES, (j + 1) * LANES)
            total = bias_ref[:, lane]
            for k in range(conv):
                at = pl.multiple_of(base + k * thoughts, thoughts)
                total = total + taps[k : k + 1, lane] * window[j, pl.ds(at, thoughts), :]
            driven = jax.nn.silu(total).astype(BF16)
            drive16[pl.ds(base, thoughts), lane] = driven
            drive_ref[j, pl.ds(base, thoughts), :] = driven.astype(F32)
        return 0

    lax.fori_loop(0, positions, convolve, 0)
    rank = live_rank(lengths, thoughts, (1, rows), 1)
    pick = (lax.broadcasted_iota(jnp.int32, (live, rows), 0) == rank).astype(F32).astype(BF16)
    kept = jnp.dot(pick, drive16[...], preferred_element_type=F32).astype(BF16)
    low = jnp.dot(kept, down_ref[...], preferred_element_type=F32).astype(BF16)
    select = jnp.dot(kept, select_ref[...], preferred_element_type=F32).astype(BF16)
    columns = low.shape[1] // LANES
    part_ref[columns * live :, :] = jnp.zeros((part_ref.shape[0] - columns * live, LANES), BF16)
    for c in range(columns):
        part_ref[c * live : (c + 1) * live, :] = low[:, c * LANES : (c + 1) * LANES]
    part_ref[columns * live : (columns + 1) * live, : select.shape[1]] = select


def greet(n, me):
    barrier = pltpu.get_barrier_semaphore()

    def one(k, _):
        pl.semaphore_signal(
            barrier, inc=1, device_id={"chan": lax.rem(me + k, n)}, device_id_type=MESH
        )
        return 0

    lax.fori_loop(1, n, one, 0)
    pl.semaphore_wait(barrier, n - 1)


def reduce_kernel(n, part_ref, out_ref, parts, whole, s_send, s_recv, g_send, g_recv):
    me = lax.axis_index("chan")
    block = part_ref.shape[0] // n
    greet(n, me)

    def rows(c):
        return pl.ds(pl.multiple_of(c * block, block), block)

    def scatter(k, there):
        return pltpu.make_async_remote_copy(
            src_ref=part_ref.at[rows(there)], dst_ref=parts.at[me],
            send_sem=s_send.at[k], recv_sem=s_recv.at[me],
            device_id={"chan": there}, device_id_type=MESH,
        )

    def gather(k, there):
        return pltpu.make_async_remote_copy(
            src_ref=whole.at[rows(me)], dst_ref=whole.at[rows(me)],
            send_sem=g_send.at[k], recv_sem=g_recv.at[me],
            device_id={"chan": there}, device_id_type=MESH,
        )

    def each(act, init=0):
        return lax.fori_loop(1, n, act, init)

    def start_scatter(k, _):
        scatter(k, lax.rem(me + k, n)).start()
        return 0

    def take(k, total):
        source = lax.rem(me + n - k, n)
        pltpu.make_async_copy(parts.at[source], parts.at[source], s_recv.at[source]).wait()
        return total + parts[source].astype(F32)

    def start_gather(k, _):
        gather(k, lax.rem(me + k, n)).start()
        return 0

    def finish(k, _):
        source, there = lax.rem(me + n - k, n), lax.rem(me + k, n)
        pltpu.make_async_copy(whole.at[rows(source)], whole.at[rows(source)], g_recv.at[source]).wait()
        scatter(k, there).wait_send()
        gather(k, there).wait_send()
        return 0

    each(start_scatter)
    total = each(take, part_ref[rows(me), :].astype(F32))
    whole[rows(me), :] = total.astype(BF16)
    each(start_gather)
    each(finish)
    out_ref[...] = whole[...]


def scan_kernel(
    fork, lengths, sums_ref, drive_ref, gate_ref, state_ref, up_ref, bias_ref, decay_ref, skip_ref,
    send_ref, rate, opened, spread, begin, decay, result, final,
):
    thoughts, positions, width = gate_ref.shape
    states = state_ref.shape[1]
    tiles, rows = width // LANES, thoughts * positions
    live = thoughts * (GEN + JUDGE // 2)
    columns = up_ref.shape[0] // LANES
    stretch = result.shape[1] // thoughts
    folds = min(4, tiles)

    def fill(t, _):
        alive = GEN + lengths[t]
        raw = gate_ref[t].astype(F32)
        keep = lax.broadcasted_iota(jnp.int32, (positions, 1), 0) < alive
        gate = jnp.where(keep, jax.nn.silu(raw), 0.0)
        first = state_ref[fork[t]]
        for j in range(tiles):
            lane = slice(j * LANES, (j + 1) * LANES)
            opened[j, pl.ds(t, positions, stride=thoughts), :] = gate[:, lane]
            begin[j, pl.ds(t, states, stride=thoughts), :] = first[:, lane]
        return 0

    lax.fori_loop(0, thoughts, fill, 0)
    scaled = jnp.exp(decay_ref[...]) * (-math.log2(math.e))
    for j in range(tiles):
        for s in range(states):
            decay[j, s * 8 : (s + 1) * 8, :] = jnp.broadcast_to(
                scaled[s : s + 1, j * LANES : (j + 1) * LANES], (8, LANES)
            )
    rank = live_rank(lengths, thoughts, (rows, 1), 0)
    place = (lax.broadcasted_iota(jnp.int32, (rows, live), 1) == rank).astype(F32).astype(BF16)
    alive = (rank >= 0).astype(F32)
    low = jnp.concatenate([sums_ref[c * live : (c + 1) * live, :] for c in range(columns)], axis=1)
    low = jnp.dot(place, low, preferred_element_type=F32).astype(BF16)
    select = jnp.dot(
        place, sums_ref[columns * live : (columns + 1) * live, :], preferred_element_type=F32
    )
    for s in range(2 * states):
        spread[s] = jnp.broadcast_to(select[:, s : s + 1], (rows, LANES))
    for j in range(tiles):
        lane = slice(j * LANES, (j + 1) * LANES)
        raw = jnp.dot(low, up_ref[:, lane], preferred_element_type=F32) + bias_ref[:, lane]
        soft = jnp.maximum(raw, 0.0) + jnp.log1p(jnp.exp(-jnp.abs(raw)))
        rate[j] = soft * alive

    def one_block(index, _):
        half, j = index // tiles, lax.rem(index, tiles)
        first = half * 8
        h = tuple(
            begin[j, pl.ds(pl.multiple_of(s * thoughts + first, 8), 8), :] for s in range(states)
        )
        skip = skip_ref[j]

        def step(p, h):
            at = pl.ds(pl.multiple_of(p * thoughts + first, 8), 8)
            step_rate, inflow = rate[j, at, :], drive_ref[j, at, :]
            push = step_rate * inflow
            later, readout = [], skip * inflow
            for s in range(states):
                factor = jnp.exp2(step_rate * decay[j, s * 8 : (s + 1) * 8, :])
                now = factor * h[s] + push * spread[s, at, :]
                readout = readout + spread[states + s, at, :] * now
                later.append(now)
            result[j, pl.ds(first * stretch + p, 8, stride=stretch), :] = readout * opened[j, at, :]
            return tuple(later)

        h = lax.fori_loop(0, positions, step, h, unroll=4)
        for s in range(states):
            final[j, pl.ds(first * states + s, 8, stride=states), :] = h[s]
        return 0

    lax.fori_loop(0, thoughts // 8 * tiles, one_block, 0)

    def pack(t, _):
        at = pl.multiple_of(t * stretch, 8)
        for j in range(tiles):
            send_ref[t, :, j * LANES : (j + 1) * LANES] = result[j, pl.ds(at, 16), :].astype(BF16)
            send_ref[t, :, width + j * LANES : width + (j + 1) * LANES] = final[
                j, pl.ds(pl.multiple_of(t * states, 8), states), :
            ].astype(BF16)
        each = tiles // folds
        for i in range(each):
            pieces = [
                result[a * each + i, pl.ds(pl.multiple_of(at + 16, 8), 8), :][: positions - 16]
                for a in range(folds)
            ]
            if folds < 4:
                pieces.append(jnp.zeros((16 - 4 * folds, LANES), F32))
            send_ref[t, :, 2 * width + i * LANES : 2 * width + (i + 1) * LANES] = jnp.concatenate(
                pieces, axis=0
            ).astype(BF16)
        return 0

    lax.fori_loop(0, thoughts, pack, 0)


def exchange_kernel(n, width, folds, send_ref, out_ref, final_ref, got, s_send, s_recv, s_own):
    me = lax.axis_index("chan")
    each = send_ref.shape[0] // n
    positions = out_ref.shape[1]
    greet(n, me)

    def mine(c):
        return pl.ds(c * each, each)

    def copy(k, there):
        return pltpu.make_async_remote_copy(
            src_ref=send_ref.at[mine(there)], dst_ref=got.at[me],
            send_sem=s_send.at[k], recv_sem=s_recv.at[me],
            device_id={"chan": there}, device_id_type=MESH,
        )

    def start(k, _):
        copy(k, lax.rem(me + k, n)).start()
        return 0

    lax.fori_loop(1, n, start, 0)
    own = pltpu.make_async_copy(send_ref.at[mine(me)], got.at[me], s_own)
    own.start()
    own.wait()

    def place(k, _):
        source = lax.rem(me + n - k, n)

        @pl.when(k > 0)
        def _():
            pltpu.make_async_copy(got.at[source], got.at[source], s_recv.at[source]).wait()

        at = pl.ds(pl.multiple_of(source * width, LANES), width)
        for i in range(each):
            head = got[source, i, :, :width].astype(F32)
            tail = got[source, i, :, 2 * width :].astype(F32)
            tail = jnp.concatenate([tail[4 * a : 4 * a + positions - 16] for a in range(folds)], axis=1)
            out_ref[i, :, at] = jnp.concatenate([head, tail], axis=0).astype(BF16)
            final_ref[i, :, at] = got[source, i, :, width : 2 * width].astype(F32)
        return 0

    lax.fori_loop(0, n, place, 0)

    def drain(k, _):
        copy(k, lax.rem(me + k, n)).wait_send()
        return 0

    lax.fori_loop(1, n, drain, 0)


def vmem(count):
    return [pl.BlockSpec(memory_space=pltpu.VMEM)] * count


def smem(count):
    return [pl.BlockSpec(memory_space=pltpu.SMEM)] * count


def body(
    parent_state,
    parent_conv,
    fork_map,
    judge_lengths,
    mixer_input,
    gate_input,
    conv_weight,
    conv_bias,
    rate_down,
    selection_weight,
    rate_up,
    rate_bias,
    decay_log,
    skip_gain,
):
    n = lax.axis_size("chan")
    thoughts, positions, width = mixer_input.shape
    states, rank = parent_state.shape[1], rate_up.shape[0]
    tiles, rows = width // LANES, thoughts * positions
    live = thoughts * (GEN + JUDGE // 2)
    used = (rank // LANES + 1) * live
    block = -(-used // (16 * n)) * 16
    folds = min(4, tiles)
    each = thoughts // n
    conv = conv_weight.shape[0]
    plain = pltpu.CompilerParams(vmem_limit_bytes=VMEM_LIMIT)

    part, driven = pl.pallas_call(
        project_kernel,
        out_shape=(
            jax.ShapeDtypeStruct((n * block, LANES), BF16),
            jax.ShapeDtypeStruct((tiles, rows, LANES), F32),
        ),
        in_specs=smem(2) + vmem(6),
        out_specs=tuple(vmem(2)),
        scratch_shapes=[
            pltpu.VMEM((tiles, (positions + conv - 1) * thoughts, LANES), F32),
            pltpu.VMEM((rows, width), BF16),
        ],
        compiler_params=plain,
        name="project",
    )(fork_map, judge_lengths, mixer_input, parent_conv, conv_weight, conv_bias[None, :],
      rate_down, selection_weight)

    sums = pl.pallas_call(
        functools.partial(reduce_kernel, n),
        out_shape=jax.ShapeDtypeStruct((n * block, LANES), BF16),
        in_specs=vmem(1),
        out_specs=vmem(1)[0],
        scratch_shapes=[
            pltpu.VMEM((n, block, LANES), BF16),
            pltpu.VMEM((n * block, LANES), BF16),
        ] + [pltpu.SemaphoreType.DMA((n,))] * 4,
        compiler_params=pltpu.CompilerParams(
            collective_id=0, has_side_effects=True, vmem_limit_bytes=VMEM_LIMIT
        ),
        name="reduce",
    )(part)

    skip = jnp.broadcast_to(skip_gain.reshape(tiles, 1, LANES), (tiles, 8, LANES))
    packed = 2 * width + width // folds
    send = pl.pallas_call(
        scan_kernel,
        out_shape=jax.ShapeDtypeStruct((thoughts, 16, packed), BF16),
        in_specs=smem(2) + vmem(8),
        out_specs=vmem(1)[0],
        scratch_shapes=[
            pltpu.VMEM((tiles, rows, LANES), F32),
            pltpu.VMEM((tiles, rows, LANES), F32),
            pltpu.VMEM((2 * states, rows, LANES), F32),
            pltpu.VMEM((tiles, states * thoughts, LANES), F32),
            pltpu.VMEM((tiles, states * 8, LANES), F32),
            pltpu.VMEM((tiles, thoughts * 24, LANES), F32),
            pltpu.VMEM((tiles, thoughts * states, LANES), F32),
        ],
        compiler_params=plain,
        name="scan",
    )(fork_map, judge_lengths, sums, driven, gate_input, parent_state, rate_up,
      rate_bias[None, :], decay_log, skip)

    return pl.pallas_call(
        functools.partial(exchange_kernel, n, width, folds),
        out_shape=(
            jax.ShapeDtypeStruct((each, positions, n * width), BF16),
            jax.ShapeDtypeStruct((each, states, n * width), F32),
        ),
        in_specs=vmem(1),
        out_specs=tuple(vmem(2)),
        scratch_shapes=[
            pltpu.VMEM((n, each, 16, packed), BF16),
            pltpu.SemaphoreType.DMA((n,)),
            pltpu.SemaphoreType.DMA((n,)),
            pltpu.SemaphoreType.DMA,
        ],
        compiler_params=pltpu.CompilerParams(
            collective_id=1, has_side_effects=True, vmem_limit_bytes=VMEM_LIMIT
        ),
        name="exchange",
    )(send)


def solution(mesh):
    placed = (
        P("group", None, "chan"),
        P("group", None, "chan"),
        P("group"),
        P("group"),
        P("group", None, "chan"),
        P("group", None, "chan"),
        P(None, "chan"),
        P("chan"),
        P("chan", None),
        P("chan", None),
        P(None, "chan"),
        P("chan"),
        P(None, "chan"),
        P("chan"),
    )
    return jax.shard_map(
        body,
        mesh=mesh,
        in_specs=placed,
        out_specs=(P(("group", "chan"), None, None), P(("group", "chan"), None, None)),
        check_vma=False,
    )
```

```python
import functools
import math

import jax
import jax.numpy as jnp
from jax import lax
from jax.experimental import pallas as pl
from jax.experimental.pallas import tpu as pltpu
from jax.sharding import PartitionSpec as P

GEN = 4
JUDGE = 16
LANES = 128
MESH = pl.DeviceIdType.MESH
F32 = jnp.float32
BF16 = jnp.bfloat16
VMEM_LIMIT = 56 * 1024 * 1024


def live_rank(lengths, thoughts, shape, axis):
    row = lax.broadcasted_iota(jnp.int32, shape, axis)
    thought = jnp.bitwise_and(row, thoughts - 1)
    position = jnp.right_shift(row, int(math.log2(thoughts)))

    def one(t, carried):
        rank, start = carried
        alive = GEN + lengths[t]
        hit = (thought == t) & (position < alive)
        return jnp.where(hit, start + position, rank), start + alive

    return lax.fori_loop(0, thoughts, one, (jnp.full(shape, -1, jnp.int32), jnp.int32(0)))[0]


def project_kernel(
    fork, lengths, x_ref, start_ref, taps_ref, bias_ref, down_ref, select_ref, part, driven, drive,
):
    positions, thoughts, width = x_ref.shape
    parents = start_ref.shape[1]
    tiles, rows = width // LANES, thoughts * positions
    conv = taps_ref.shape[0]
    live = thoughts * (GEN + JUDGE // 2)
    columns = down_ref.shape[1] // LANES
    lanes = [slice(j * LANES, (j + 1) * LANES) for j in range(tiles)]

    shape = (thoughts, parents)
    row, col = lax.broadcasted_iota(jnp.int32, shape, 0), lax.broadcasted_iota(jnp.int32, shape, 1)
    picked = lax.fori_loop(
        0, thoughts,
        lambda t, now: jnp.where((row == t) & (col == fork[t]), 1.0, now),
        jnp.zeros(shape, F32),
    ).astype(BF16)
    taps = taps_ref[...].astype(F32)
    before = [jnp.dot(picked, start_ref[k], preferred_element_type=F32) for k in range(conv - 1)]
    for p in range(positions):
        total = bias_ref[...]
        for k in range(conv):
            at = p + k - (conv - 1)
            value = before[at + conv - 1] if at < 0 else x_ref[at].astype(F32)
            total = total + taps[k : k + 1] * value
        value = jax.nn.silu(total).astype(BF16)
        drive[p * thoughts : (p + 1) * thoughts, :] = value
        for j in range(tiles):
            driven[j, p * thoughts : (p + 1) * thoughts, :] = value[:, lanes[j]].astype(F32)

    rank_row = live_rank(lengths, thoughts, (1, rows), 1)
    pick = (lax.broadcasted_iota(jnp.int32, (live, rows), 0) == rank_row).astype(F32).astype(BF16)
    kept = jnp.dot(pick, drive[...], preferred_element_type=F32).astype(BF16)
    low = jnp.dot(kept, down_ref[...], preferred_element_type=F32).astype(BF16)
    select = lax.dot_general(
        kept, select_ref[...], (((1,), (1,)), ((), ())), preferred_element_type=F32
    ).astype(BF16)
    part[columns * live :, :] = jnp.zeros((part.shape[0] - columns * live, LANES), BF16)
    for c in range(columns):
        part[c * live : (c + 1) * live, :] = low[:, c * LANES : (c + 1) * LANES]
    part[columns * live : (columns + 1) * live, : select.shape[1]] = select


def greet(n, me):
    barrier = pltpu.get_barrier_semaphore()

    def one(k, _):
        pl.semaphore_signal(
            barrier, inc=1, device_id={"chan": lax.rem(me + k, n)}, device_id_type=MESH
        )
        return 0

    lax.fori_loop(1, n, one, 0)
    pl.semaphore_wait(barrier, n - 1)


def reduce_kernel(n, part_ref, out_ref, parts, whole, s_send, s_recv, g_send, g_recv):
    me = lax.axis_index("chan")
    block = part_ref.shape[0] // n
    greet(n, me)

    def rows(c):
        return pl.ds(pl.multiple_of(c * block, block), block)

    def scatter(k, there):
        return pltpu.make_async_remote_copy(
            src_ref=part_ref.at[rows(there)], dst_ref=parts.at[me],
            send_sem=s_send.at[k], recv_sem=s_recv.at[me],
            device_id={"chan": there}, device_id_type=MESH,
        )

    def gather(k, there):
        return pltpu.make_async_remote_copy(
            src_ref=whole.at[rows(me)], dst_ref=whole.at[rows(me)],
            send_sem=g_send.at[k], recv_sem=g_recv.at[me],
            device_id={"chan": there}, device_id_type=MESH,
        )

    def each(act, init=0):
        return lax.fori_loop(1, n, act, init)

    def start_scatter(k, _):
        scatter(k, lax.rem(me + k, n)).start()
        return 0

    def take(k, total):
        source = lax.rem(me + n - k, n)
        pltpu.make_async_copy(parts.at[source], parts.at[source], s_recv.at[source]).wait()
        return total + parts[source].astype(F32)

    def start_gather(k, _):
        gather(k, lax.rem(me + k, n)).start()
        return 0

    def finish(k, _):
        source, there = lax.rem(me + n - k, n), lax.rem(me + k, n)
        pltpu.make_async_copy(whole.at[rows(source)], whole.at[rows(source)], g_recv.at[source]).wait()
        scatter(k, there).wait_send()
        gather(k, there).wait_send()
        return 0

    each(start_scatter)
    total = each(take, part_ref[rows(me), :].astype(F32))
    whole[rows(me), :] = total.astype(BF16)
    each(start_gather)
    each(finish)
    out_ref[...] = whole[...]


def scan_kernel(
    n, fork, lengths, whole, driven, gate_ref, state_ref, up_ref, rate_bias_ref, decay_ref, skip_ref,
    got_ref,
    alive, opened, begin, decay, rate, spread, result, final,
    x_send, x_recv, x_own, *sends,
):
    positions, thoughts, width = gate_ref.shape
    states = state_ref.shape[1]
    tiles, rows = width // LANES, thoughts * positions
    live = thoughts * (GEN + JUDGE // 2)
    columns = up_ref.shape[0] // LANES
    stretch = result.shape[1] // thoughts
    folds = min(4, tiles)
    lanes = [slice(j * LANES, (j + 1) * LANES) for j in range(tiles)]
    me = lax.axis_index("chan")
    barrier = pltpu.get_barrier_semaphore()

    def greet(k, _):
        pl.semaphore_signal(
            barrier, inc=1, device_id={"chan": lax.rem(me + k, n)}, device_id_type=MESH
        )
        return 0

    lax.fori_loop(1, n, greet, 0)

    rank = live_rank(lengths, thoughts, (rows, 1), 0)
    place = (lax.broadcasted_iota(jnp.int32, (rows, live), 1) == rank).astype(F32).astype(BF16)
    alive[...] = jnp.broadcast_to((rank >= 0).astype(F32), (rows, LANES))
    def fill(t, _):
        first = state_ref[fork[t]]
        for j in range(tiles):
            begin[j, pl.ds(t, states, stride=thoughts), :] = first[:, lanes[j]]
        return 0

    lax.fori_loop(0, thoughts, fill, 0)

    def open_gate(p, _):
        at = pl.ds(pl.multiple_of(p * thoughts, 8), thoughts)
        gate = jax.nn.silu(gate_ref[p].astype(F32))
        for j in range(tiles):
            opened[j, at, :] = jnp.where(alive[at, :] > 0.0, gate[:, lanes[j]], 0.0)
        return 0

    lax.fori_loop(0, positions, open_gate, 0)
    scaled = jnp.exp(decay_ref[...]) * (-math.log2(math.e))
    for j in range(tiles):
        for s in range(states):
            decay[j, s * 8 : (s + 1) * 8, :] = jnp.broadcast_to(
                scaled[s : s + 1, lanes[j]], (8, LANES)
            )

    low = jnp.concatenate([whole[c * live : (c + 1) * live, :] for c in range(columns)], axis=1)
    low = jnp.dot(place, low, preferred_element_type=F32).astype(BF16)
    select = jnp.dot(
        place, whole[columns * live : (columns + 1) * live, :], preferred_element_type=F32
    )
    for s in range(2 * states):
        spread[s] = jnp.broadcast_to(select[:, s : s + 1], (rows, LANES))
    for j in range(tiles):
        raw = jnp.dot(low, up_ref[:, lanes[j]], preferred_element_type=F32)
        raw = raw + rate_bias_ref[:, lanes[j]]
        soft = jnp.maximum(raw, 0.0) + jnp.log1p(jnp.exp(-jnp.abs(raw)))
        rate[j] = soft * alive[...]

    pl.semaphore_wait(barrier, n - 1)

    def remote(source, target, sent, received, there):
        return pltpu.make_async_remote_copy(
            src_ref=source, dst_ref=target, send_sem=sent, recv_sem=received,
            device_id={"chan": there}, device_id_type=MESH,
        )

    def arrived(where, semaphore):
        pltpu.make_async_copy(where, where, semaphore).wait()

    each = thoughts // n
    groups, owners = thoughts // 8, 8 // each
    group = (me * each) // 8

    def exchange(i, q):
        now_group = lax.rem(group + groups // 2 + i, groups)
        return remote(
            sends[i].at[pl.ds(q * each, each)], got_ref.at[me], x_send.at[i * owners + q],
            x_recv.at[me], now_group * owners + q,
        )

    own_slot = lax.rem(me, owners)
    own_copy = pltpu.make_async_copy(
        sends[-(groups // 2) % groups].at[pl.ds(own_slot * each, each)], got_ref.at[me], x_own
    )

    def one_group(i):
        now_group = lax.rem(group + groups // 2 + i, groups)
        send = sends[i]
        first = pl.multiple_of(now_group * 8, 8)

        def one_block(pair, _):
            js = [pair * 2 + m for m in range(2)]
            h = tuple(
                begin[j, pl.ds(pl.multiple_of(s * thoughts + first, 8), 8), :]
                for s in range(states) for j in js
            )
            skips = [skip_ref[j] for j in js]

            def step(p, h):
                at = pl.ds(pl.multiple_of(p * thoughts + first, 8), 8)
                rates = [rate[j, at, :] for j in js]
                inflows = [driven[j, at, :] for j in js]
                pushes = [a * b for a, b in zip(rates, inflows)]
                readouts = [a * b for a, b in zip(skips, inflows)]
                later = []
                for s in range(states):
                    into, out = spread[s, at, :], spread[states + s, at, :]
                    for m in range(2):
                        factor = jnp.exp2(rates[m] * decay[js[m], s * 8 : (s + 1) * 8, :])
                        now = factor * h[2 * s + m] + pushes[m] * into
                        readouts[m] = readouts[m] + out * now
                        later.append(now)
                for m in range(2):
                    result[js[m], pl.ds(first * stretch + p, 8, stride=stretch), :] = (
                        readouts[m] * opened[js[m], at, :]
                    )
                return tuple(later)

            h = lax.fori_loop(0, positions, step, h, unroll=2)
            for s in range(states):
                for m in range(2):
                    final[js[m], pl.ds(first * states + s, 8, stride=states), :] = h[2 * s + m]
            return 0

        lax.fori_loop(0, tiles // 2, one_block, 0)

        def pack(slot, _):
            t = first + slot
            at = pl.multiple_of(t * stretch, 8)
            for j in range(tiles):
                send[slot, :, lanes[j]] = result[j, pl.ds(at, 16), :].astype(BF16)
                send[slot, :, width + j * LANES : width + (j + 1) * LANES] = final[
                    j, pl.ds(pl.multiple_of(t * states, 8), states), :
                ].astype(BF16)
            apart = tiles // folds
            for i in range(apart):
                pieces = [
                    result[a * apart + i, pl.ds(pl.multiple_of(at + 16, 8), 8), :][: positions - 16]
                    for a in range(folds)
                ]
                if folds < 4:
                    pieces.append(jnp.zeros((16 - 4 * folds, LANES), F32))
                send[slot, :, 2 * width + i * LANES : 2 * width + (i + 1) * LANES] = jnp.concatenate(
                    pieces, axis=0
                ).astype(BF16)
            return 0

        lax.fori_loop(0, 8, pack, 0)

        def dispatch(k, _):
            q = lax.rem(me + k, owners)

            @pl.when(now_group * owners + q != me)
            def _():
                exchange(i, q).start()

            return 0

        lax.fori_loop(0, owners, dispatch, 0)
        if i == -(groups // 2) % groups:
            own_copy.start()

    for i in range(groups):
        one_group(i)

    def drain_exchange(k, _):
        source = lax.rem(me + k, n)
        arrived(got_ref.at[source], x_recv.at[source])
        return 0

    for i in range(groups):
        def drain_send(q, _):
            @pl.when(lax.rem(group + groups // 2 + i, groups) * owners + q != me)
            def _():
                exchange(i, q).wait_send()

            return 0

        lax.fori_loop(0, owners, drain_send, 0)

    own_copy.wait()
    lax.fori_loop(1, n, drain_exchange, 0)


def unfold_kernel(folds, got_ref, out_ref, final_ref):
    sources, each = got_ref.shape[:2]
    positions = out_ref.shape[1]
    width = out_ref.shape[2] // sources
    for c in range(sources):
        at = slice(c * width, (c + 1) * width)
        for i in range(each):
            head = got_ref[c, i, :, :width].astype(F32)
            tail = got_ref[c, i, :, 2 * width :].astype(F32)
            tail = jnp.concatenate(
                [tail[4 * a : 4 * a + positions - 16] for a in range(folds)], axis=1
            )
            out_ref[i, :, at] = jnp.concatenate([head, tail], axis=0).astype(BF16)
            final_ref[i, :, at] = got_ref[c, i, :, width : 2 * width].astype(F32)


def vmem(count):
    return [pl.BlockSpec(memory_space=pltpu.VMEM)] * count


def smem(count):
    return [pl.BlockSpec(memory_space=pltpu.SMEM)] * count


def body(
    parent_state,
    parent_conv,
    fork_map,
    judge_lengths,
    mixer_input,
    gate_input,
    conv_weight,
    conv_bias,
    rate_down,
    selection_weight,
    rate_up,
    rate_bias,
    decay_log,
    skip_gain,
):
    n = lax.axis_size("chan")
    thoughts, positions, width = mixer_input.shape
    states, rank = parent_state.shape[1], rate_up.shape[0]
    tiles, rows = width // LANES, thoughts * positions
    live = thoughts * (GEN + JUDGE // 2)
    used = (rank // LANES + 1) * live
    block = -(-used // (16 * n)) * 16
    folds = min(4, tiles)
    each = thoughts // n
    packed = 2 * width + width // folds
    skip = jnp.broadcast_to(skip_gain.reshape(tiles, 1, LANES), (tiles, 8, LANES))
    dma = pltpu.SemaphoreType.DMA

    remote = functools.partial(
        pltpu.CompilerParams, has_side_effects=True, vmem_limit_bytes=VMEM_LIMIT
    )
    part, driven = pl.pallas_call(
        project_kernel,
        out_shape=(
            jax.ShapeDtypeStruct((n * block, LANES), BF16),
            jax.ShapeDtypeStruct((tiles, rows, LANES), F32),
        ),
        in_specs=smem(2) + vmem(6),
        out_specs=tuple(vmem(2)),
        scratch_shapes=[pltpu.VMEM((rows, width), BF16)],
        compiler_params=pltpu.CompilerParams(vmem_limit_bytes=VMEM_LIMIT),
        name="project",
    )(fork_map, judge_lengths, jnp.swapaxes(mixer_input, 0, 1), jnp.swapaxes(parent_conv, 0, 1),
      conv_weight, conv_bias[None, :], rate_down, selection_weight.T)

    sums = pl.pallas_call(
        functools.partial(reduce_kernel, n),
        out_shape=jax.ShapeDtypeStruct((n * block, LANES), BF16),
        in_specs=vmem(1),
        out_specs=vmem(1)[0],
        scratch_shapes=[
            pltpu.VMEM((n, block, LANES), BF16),
            pltpu.VMEM((n * block, LANES), BF16),
        ] + [dma((n,))] * 4,
        compiler_params=remote(collective_id=0),
        name="reduce",
    )(part)

    got = pl.pallas_call(
        functools.partial(scan_kernel, n),
        out_shape=jax.ShapeDtypeStruct((n, each, 16, packed), BF16),
        in_specs=smem(2) + vmem(8),
        out_specs=pl.BlockSpec(memory_space=pl.ANY),
        scratch_shapes=[
            pltpu.VMEM((rows, LANES), F32),
            pltpu.VMEM((tiles, rows, LANES), F32),
            pltpu.VMEM((tiles, states * thoughts, LANES), F32),
            pltpu.VMEM((tiles, states * 8, LANES), F32),
            pltpu.VMEM((tiles, rows, LANES), F32),
            pltpu.VMEM((2 * states, rows, LANES), F32),
            pltpu.VMEM((tiles, thoughts * 24, LANES), F32),
            pltpu.VMEM((tiles, thoughts * states, LANES), F32),
        ] + [dma((n,))] * 2 + [dma]
        + [pltpu.VMEM((8, 16, packed), BF16)] * (thoughts // 8),
        compiler_params=remote(collective_id=1),
        name="scan",
    )(fork_map, judge_lengths, sums, driven, jnp.swapaxes(gate_input, 0, 1), parent_state,
      rate_up, rate_bias[None, :], decay_log, skip)

    together = n // 4
    return pl.pallas_call(
        functools.partial(unfold_kernel, folds),
        grid=(n // together,),
        out_shape=(
            jax.ShapeDtypeStruct((each, positions, n * width), BF16),
            jax.ShapeDtypeStruct((each, states, n * width), F32),
        ),
        in_specs=[pl.BlockSpec((together, each, 16, packed), lambda c: (c, 0, 0, 0))],
        out_specs=(
            pl.BlockSpec((each, positions, together * width), lambda c: (0, 0, c)),
            pl.BlockSpec((each, states, together * width), lambda c: (0, 0, c)),
        ),
        compiler_params=pltpu.CompilerParams(vmem_limit_bytes=VMEM_LIMIT),
        name="unfold",
    )(got)


def solution(mesh):
    placed = (
        P("group", None, "chan"),
        P("group", None, "chan"),
        P("group"),
        P("group"),
        P("group", None, "chan"),
        P("group", None, "chan"),
        P(None, "chan"),
        P("chan"),
        P("chan", None),
        P("chan", None),
        P(None, "chan"),
        P("chan"),
        P(None, "chan"),
        P("chan"),
    )
    return jax.shard_map(
        body,
        mesh=mesh,
        in_specs=placed,
        out_specs=(P(("group", "chan"), None, None), P(("group", "chan"), None, None)),
        check_vma=False,
    )
```

```python
import functools
import math

import jax
import jax.numpy as jnp
from jax import lax
from jax.experimental import pallas as pl
from jax.experimental.pallas import tpu as pltpu
from jax.sharding import PartitionSpec as P

GEN = 4
JUDGE = 16
LANES = 128
MESH = pl.DeviceIdType.MESH
F32 = jnp.float32
BF16 = jnp.bfloat16
VMEM_LIMIT = 56 * 1024 * 1024


def live_rank(lengths, thoughts, shape, axis):
    row = lax.broadcasted_iota(jnp.int32, shape, axis)
    thought = jnp.bitwise_and(row, thoughts - 1)
    position = jnp.right_shift(row, int(math.log2(thoughts)))

    def one(t, carried):
        rank, start = carried
        alive = GEN + lengths[t]
        hit = (thought == t) & (position < alive)
        return jnp.where(hit, start + position, rank), start + alive

    return lax.fori_loop(0, thoughts, one, (jnp.full(shape, -1, jnp.int32), jnp.int32(0)))[0]


def mixer_kernel(
    n, fork, lengths, x_ref, start_ref, taps_ref, bias_ref, down_ref, select_ref,
    gate_ref, state_ref, up_ref, rate_bias_ref, decay_ref, skip_ref,
    got_ref,
    drive, driven, part, parts, whole, alive, opened, begin, decay, rate, spread,
    result, final, s_send, s_recv, g_send, g_recv, x_send, x_recv, x_own, *sends,
):
    positions, thoughts, width = x_ref.shape
    states, parents = state_ref.shape[1], state_ref.shape[0]
    tiles, rows = width // LANES, thoughts * positions
    conv = taps_ref.shape[0]
    live = thoughts * (GEN + JUDGE // 2)
    columns = up_ref.shape[0] // LANES
    stretch = result.shape[1] // thoughts
    folds = min(4, tiles)
    lanes = [slice(j * LANES, (j + 1) * LANES) for j in range(tiles)]
    me = lax.axis_index("chan")
    block = part.shape[0] // n

    barrier = pltpu.get_barrier_semaphore()

    def greet(k, _):
        pl.semaphore_signal(
            barrier, inc=1, device_id={"chan": lax.rem(me + k, n)}, device_id_type=MESH
        )
        return 0

    lax.fori_loop(1, n, greet, 0)

    shape = (thoughts, parents)
    row, col = lax.broadcasted_iota(jnp.int32, shape, 0), lax.broadcasted_iota(jnp.int32, shape, 1)
    picked = lax.fori_loop(
        0, thoughts,
        lambda t, now: jnp.where((row == t) & (col == fork[t]), 1.0, now),
        jnp.zeros(shape, F32),
    ).astype(BF16)
    taps = taps_ref[...].astype(F32)
    before = [jnp.dot(picked, start_ref[k], preferred_element_type=F32) for k in range(conv - 1)]
    for p in range(positions):
        total = bias_ref[...]
        for k in range(conv):
            at = p + k - (conv - 1)
            value = before[at + conv - 1] if at < 0 else x_ref[at].astype(F32)
            total = total + taps[k : k + 1] * value
        value = jax.nn.silu(total).astype(BF16)
        drive[p * thoughts : (p + 1) * thoughts, :] = value
        for j in range(tiles):
            driven[j, p * thoughts : (p + 1) * thoughts, :] = value[:, lanes[j]].astype(F32)

    rank_row = live_rank(lengths, thoughts, (1, rows), 1)
    pick = (lax.broadcasted_iota(jnp.int32, (live, rows), 0) == rank_row).astype(F32).astype(BF16)
    kept = jnp.dot(pick, drive[...], preferred_element_type=F32).astype(BF16)
    low = jnp.dot(kept, down_ref[...], preferred_element_type=F32).astype(BF16)
    select = lax.dot_general(
        kept, select_ref[...], (((1,), (1,)), ((), ())), preferred_element_type=F32
    ).astype(BF16)
    part[columns * live :, :] = jnp.zeros((part.shape[0] - columns * live, LANES), BF16)
    for c in range(columns):
        part[c * live : (c + 1) * live, :] = low[:, c * LANES : (c + 1) * LANES]
    part[columns * live : (columns + 1) * live, : select.shape[1]] = select

    pl.semaphore_wait(barrier, n - 1)

    def rows_of(c):
        return pl.ds(pl.multiple_of(c * block, 16), block)

    def remote(source, target, sent, received, there):
        return pltpu.make_async_remote_copy(
            src_ref=source, dst_ref=target, send_sem=sent, recv_sem=received,
            device_id={"chan": there}, device_id_type=MESH,
        )

    def arrived(where, semaphore):
        pltpu.make_async_copy(where, where, semaphore).wait()

    def scatter(k):
        there = lax.rem(me + k, n)
        return remote(part.at[rows_of(there)], parts.at[me], s_send.at[k], s_recv.at[me], there)

    def gather(k):
        mine = whole.at[rows_of(me)]
        return remote(mine, mine, g_send.at[k], g_recv.at[me], lax.rem(me + k, n))

    def start_scatter(k, _):
        scatter(k).start()
        return 0

    lax.fori_loop(1, n, start_scatter, 0)
    rank = live_rank(lengths, thoughts, (rows, 1), 0)
    place = (lax.broadcasted_iota(jnp.int32, (rows, live), 1) == rank).astype(F32).astype(BF16)
    alive[...] = jnp.broadcast_to((rank >= 0).astype(F32), (rows, LANES))

    def fill(t, _):
        first = state_ref[fork[t]]
        for j in range(tiles):
            begin[j, pl.ds(t, states, stride=thoughts), :] = first[:, lanes[j]]
        return 0

    lax.fori_loop(0, thoughts, fill, 0)

    scaled = jnp.exp(decay_ref[...]) * (-math.log2(math.e))
    for j in range(tiles):
        for s in range(states):
            decay[j, s * 8 : (s + 1) * 8, :] = jnp.broadcast_to(
                scaled[s : s + 1, lanes[j]], (8, LANES)
            )

    def take(k, total):
        source = lax.rem(me + n - k, n)
        arrived(parts.at[source], s_recv.at[source])
        return total + parts[source].astype(F32)

    total = lax.fori_loop(1, n, take, part[rows_of(me), :].astype(F32))
    whole[rows_of(me), :] = total.astype(BF16)

    def start_gather(k, _):
        gather(k).start()
        return 0

    lax.fori_loop(1, n, start_gather, 0)

    def open_gate(p, _):
        at = pl.ds(pl.multiple_of(p * thoughts, 8), thoughts)
        gate = jax.nn.silu(gate_ref[p].astype(F32))
        for j in range(tiles):
            opened[j, at, :] = jnp.where(alive[at, :] > 0.0, gate[:, lanes[j]], 0.0)
        return 0

    lax.fori_loop(0, positions, open_gate, 0)
    def take_sum(k, _):
        source = lax.rem(me + n - k, n)
        arrived(whole.at[rows_of(source)], g_recv.at[source])
        return 0

    lax.fori_loop(1, n, take_sum, 0)

    low = jnp.concatenate([whole[c * live : (c + 1) * live, :] for c in range(columns)], axis=1)
    low = jnp.dot(place, low, preferred_element_type=F32).astype(BF16)
    select = jnp.dot(
        place, whole[columns * live : (columns + 1) * live, :], preferred_element_type=F32
    )
    for s in range(2 * states):
        spread[s] = jnp.broadcast_to(select[:, s : s + 1], (rows, LANES))
    for j in range(tiles):
        raw = jnp.dot(low, up_ref[:, lanes[j]], preferred_element_type=F32)
        raw = raw + rate_bias_ref[:, lanes[j]]
        soft = jnp.maximum(raw, 0.0) + jnp.log1p(jnp.exp(-jnp.abs(raw)))
        rate[j] = soft * alive[...]

    each = thoughts // n
    groups, owners = thoughts // 8, 8 // each
    group = (me * each) // 8

    def exchange(i, q):
        now_group = lax.rem(group + groups // 2 + i, groups)
        return remote(
            sends[i].at[pl.ds(q * each, each)], got_ref.at[me], x_send.at[i * owners + q],
            x_recv.at[me], now_group * owners + q,
        )

    own_slot = lax.rem(me, owners)
    own_copy = pltpu.make_async_copy(
        sends[-(groups // 2) % groups].at[pl.ds(own_slot * each, each)], got_ref.at[me], x_own
    )

    def one_group(i):
        now_group = lax.rem(group + groups // 2 + i, groups)
        send = sends[i]
        first = pl.multiple_of(now_group * 8, 8)

        def one_block(pair, _):
            js = [pair * 2 + m for m in range(2)]
            h = tuple(
                begin[j, pl.ds(pl.multiple_of(s * thoughts + first, 8), 8), :]
                for s in range(states) for j in js
            )
            skips = [skip_ref[j] for j in js]

            def step(p, h):
                at = pl.ds(pl.multiple_of(p * thoughts + first, 8), 8)
                rates = [rate[j, at, :] for j in js]
                inflows = [driven[j, at, :] for j in js]
                pushes = [a * b for a, b in zip(rates, inflows)]
                readouts = [a * b for a, b in zip(skips, inflows)]
                later = []
                for s in range(states):
                    into, out = spread[s, at, :], spread[states + s, at, :]
                    for m in range(2):
                        factor = jnp.exp2(rates[m] * decay[js[m], s * 8 : (s + 1) * 8, :])
                        now = factor * h[2 * s + m] + pushes[m] * into
                        readouts[m] = readouts[m] + out * now
                        later.append(now)
                for m in range(2):
                    result[js[m], pl.ds(first * stretch + p, 8, stride=stretch), :] = (
                        readouts[m] * opened[js[m], at, :]
                    )
                return tuple(later)

            h = lax.fori_loop(0, positions, step, h, unroll=2)
            for s in range(states):
                for m in range(2):
                    final[js[m], pl.ds(first * states + s, 8, stride=states), :] = h[2 * s + m]
            return 0

        lax.fori_loop(0, tiles // 2, one_block, 0)

        def pack(slot, _):
            t = first + slot
            at = pl.multiple_of(t * stretch, 8)
            for j in range(tiles):
                send[slot, :, lanes[j]] = result[j, pl.ds(at, 16), :].astype(BF16)
                send[slot, :, width + j * LANES : width + (j + 1) * LANES] = final[
                    j, pl.ds(pl.multiple_of(t * states, 8), states), :
                ].astype(BF16)
            apart = tiles // folds
            for i in range(apart):
                pieces = [
                    result[a * apart + i, pl.ds(pl.multiple_of(at + 16, 8), 8), :][: positions - 16]
                    for a in range(folds)
                ]
                if folds < 4:
                    pieces.append(jnp.zeros((16 - 4 * folds, LANES), F32))
                send[slot, :, 2 * width + i * LANES : 2 * width + (i + 1) * LANES] = jnp.concatenate(
                    pieces, axis=0
                ).astype(BF16)
            return 0

        lax.fori_loop(0, 8, pack, 0)

        def dispatch(k, _):
            q = lax.rem(me + k, owners)

            @pl.when(now_group * owners + q != me)
            def _():
                exchange(i, q).start()

            return 0

        lax.fori_loop(0, owners, dispatch, 0)
        if i == -(groups // 2) % groups:
            own_copy.start()

    for i in range(groups):
        one_group(i)

    def drain_sums(k, _):
        scatter(k).wait_send()
        gather(k).wait_send()
        return 0

    def drain_exchange(k, _):
        source = lax.rem(me + k, n)
        arrived(got_ref.at[source], x_recv.at[source])
        return 0

    for i in range(groups):
        def drain_send(q, _):
            @pl.when(lax.rem(group + groups // 2 + i, groups) * owners + q != me)
            def _():
                exchange(i, q).wait_send()

            return 0

        lax.fori_loop(0, owners, drain_send, 0)

    lax.fori_loop(1, n, drain_sums, 0)
    own_copy.wait()
    lax.fori_loop(1, n, drain_exchange, 0)


def unfold_kernel(folds, got_ref, out_ref, final_ref):
    sources, each = got_ref.shape[:2]
    positions = out_ref.shape[1]
    width = out_ref.shape[2] // sources
    for c in range(sources):
        at = slice(c * width, (c + 1) * width)
        for i in range(each):
            head = got_ref[c, i, :, :width].astype(F32)
            tail = got_ref[c, i, :, 2 * width :].astype(F32)
            tail = jnp.concatenate(
                [tail[4 * a : 4 * a + positions - 16] for a in range(folds)], axis=1
            )
            out_ref[i, :, at] = jnp.concatenate([head, tail], axis=0).astype(BF16)
            final_ref[i, :, at] = got_ref[c, i, :, width : 2 * width].astype(F32)


def vmem(count):
    return [pl.BlockSpec(memory_space=pltpu.VMEM)] * count


def smem(count):
    return [pl.BlockSpec(memory_space=pltpu.SMEM)] * count


def body(
    parent_state,
    parent_conv,
    fork_map,
    judge_lengths,
    mixer_input,
    gate_input,
    conv_weight,
    conv_bias,
    rate_down,
    selection_weight,
    rate_up,
    rate_bias,
    decay_log,
    skip_gain,
):
    n = lax.axis_size("chan")
    thoughts, positions, width = mixer_input.shape
    states, rank = parent_state.shape[1], rate_up.shape[0]
    tiles, rows = width // LANES, thoughts * positions
    live = thoughts * (GEN + JUDGE // 2)
    used = (rank // LANES + 1) * live
    block = -(-used // (16 * n)) * 16
    folds = min(4, tiles)
    each = thoughts // n
    packed = 2 * width + width // folds
    dma = pltpu.SemaphoreType.DMA

    got = pl.pallas_call(
        functools.partial(mixer_kernel, n),
        out_shape=jax.ShapeDtypeStruct((n, each, 16, packed), BF16),
        in_specs=smem(2) + vmem(12),
        out_specs=pl.BlockSpec(memory_space=pl.ANY),
        scratch_shapes=[
            pltpu.VMEM((rows, width), BF16),
            pltpu.VMEM((tiles, rows, LANES), F32),
            pltpu.VMEM((n * block, LANES), BF16),
            pltpu.VMEM((n, block, LANES), BF16),
            pltpu.VMEM((n * block, LANES), BF16),
            pltpu.VMEM((rows, LANES), F32),
            pltpu.VMEM((tiles, rows, LANES), F32),
            pltpu.VMEM((tiles, states * thoughts, LANES), F32),
            pltpu.VMEM((tiles, states * 8, LANES), F32),
            pltpu.VMEM((tiles, rows, LANES), F32),
            pltpu.VMEM((2 * states, rows, LANES), F32),
            pltpu.VMEM((tiles, thoughts * 24, LANES), F32),
            pltpu.VMEM((tiles, thoughts * states, LANES), F32),
        ] + [dma((n,))] * 6 + [dma]
        + [pltpu.VMEM((8, 16, packed), BF16)] * (thoughts // 8),
        compiler_params=pltpu.CompilerParams(
            collective_id=0, has_side_effects=True, vmem_limit_bytes=VMEM_LIMIT
        ),
        name="mixer",
    )(fork_map, judge_lengths, jnp.swapaxes(mixer_input, 0, 1), jnp.swapaxes(parent_conv, 0, 1),
      conv_weight, conv_bias[None, :], rate_down, selection_weight.T,
      jnp.swapaxes(gate_input, 0, 1), parent_state, rate_up, rate_bias[None, :], decay_log,
      skip_gain.reshape(tiles, 1, LANES))

    together = n // 4
    return pl.pallas_call(
        functools.partial(unfold_kernel, folds),
        grid=(n // together,),
        out_shape=(
            jax.ShapeDtypeStruct((each, positions, n * width), BF16),
            jax.ShapeDtypeStruct((each, states, n * width), F32),
        ),
        in_specs=[pl.BlockSpec((together, each, 16, packed), lambda c: (c, 0, 0, 0))],
        out_specs=(
            pl.BlockSpec((each, positions, together * width), lambda c: (0, 0, c)),
            pl.BlockSpec((each, states, together * width), lambda c: (0, 0, c)),
        ),
        compiler_params=pltpu.CompilerParams(vmem_limit_bytes=VMEM_LIMIT),
        name="unfold",
    )(got)


def solution(mesh):
    placed = (
        P("group", None, "chan"),
        P("group", None, "chan"),
        P("group"),
        P("group"),
        P("group", None, "chan"),
        P("group", None, "chan"),
        P(None, "chan"),
        P("chan"),
        P("chan", None),
        P("chan", None),
        P(None, "chan"),
        P("chan"),
        P(None, "chan"),
        P("chan"),
    )
    return jax.shard_map(
        body,
        mesh=mesh,
        in_specs=placed,
        out_specs=(P(("group", "chan"), None, None), P(("group", "chan"), None, None)),
        check_vma=False,
    )
```

```python
import functools
import math

import jax
import jax.numpy as jnp
from jax import lax
from jax.experimental import pallas as pl
from jax.experimental.pallas import tpu as pltpu
from jax.sharding import PartitionSpec as P

GEN = 4
JUDGE = 16
LANES = 128
MESH = pl.DeviceIdType.MESH
F32 = jnp.float32
BF16 = jnp.bfloat16
VMEM_LIMIT = 56 * 1024 * 1024


def live_rank(lengths, thoughts, shape, axis):
    row = lax.broadcasted_iota(jnp.int32, shape, axis)
    thought = jnp.bitwise_and(row, thoughts - 1)
    position = jnp.right_shift(row, int(math.log2(thoughts)))

    def one(t, carried):
        rank, start = carried
        alive = GEN + lengths[t]
        hit = (thought == t) & (position < alive)
        return jnp.where(hit, start + position, rank), start + alive

    return lax.fori_loop(0, thoughts, one, (jnp.full(shape, -1, jnp.int32), jnp.int32(0)))[0]


def mixer_kernel(
    n, fork, lengths, x_ref, start_ref, taps_ref, bias_ref, down_ref, select_ref,
    gate_ref, state_ref, up_ref, rate_bias_ref, decay_ref, skip_ref,
    got_ref,
    drive, driven, part, parts, whole, alive, opened, begin, decay, rate, spread,
    result, final, s_send, s_recv, g_send, g_recv, x_send, x_recv, x_own, *sends,
):
    positions, thoughts, width = x_ref.shape
    states, parents = state_ref.shape[1], state_ref.shape[0]
    tiles, rows = width // LANES, thoughts * positions
    conv = taps_ref.shape[0]
    live = thoughts * (GEN + JUDGE // 2)
    columns = up_ref.shape[0] // LANES
    stretch = result.shape[1] // thoughts
    folds = min(4, tiles)
    lanes = [slice(j * LANES, (j + 1) * LANES) for j in range(tiles)]
    me = lax.axis_index("chan")
    block = part.shape[0] // n

    barrier = pltpu.get_barrier_semaphore()

    def greet(k, _):
        pl.semaphore_signal(
            barrier, inc=1, device_id={"chan": lax.rem(me + k, n)}, device_id_type=MESH
        )
        return 0

    lax.fori_loop(1, n, greet, 0)

    shape = (thoughts, parents)
    row, col = lax.broadcasted_iota(jnp.int32, shape, 0), lax.broadcasted_iota(jnp.int32, shape, 1)
    picked = lax.fori_loop(
        0, thoughts,
        lambda t, now: jnp.where((row == t) & (col == fork[t]), 1.0, now),
        jnp.zeros(shape, F32),
    ).astype(BF16)
    taps = taps_ref[...].astype(F32)
    before = [jnp.dot(picked, start_ref[k], preferred_element_type=F32) for k in range(conv - 1)]
    for p in range(positions):
        total = bias_ref[...]
        for k in range(conv):
            at = p + k - (conv - 1)
            value = before[at + conv - 1] if at < 0 else x_ref[at].astype(F32)
            total = total + taps[k : k + 1] * value
        value = jax.nn.silu(total).astype(BF16)
        drive[p * thoughts : (p + 1) * thoughts, :] = value
        for j in range(tiles):
            driven[j, p * thoughts : (p + 1) * thoughts, :] = value[:, lanes[j]].astype(F32)

    rank_row = live_rank(lengths, thoughts, (1, rows), 1)
    pick = (lax.broadcasted_iota(jnp.int32, (live, rows), 0) == rank_row).astype(F32).astype(BF16)
    kept = jnp.dot(pick, drive[...], preferred_element_type=F32).astype(BF16)
    low = jnp.dot(kept, down_ref[...], preferred_element_type=F32).astype(BF16)
    select = lax.dot_general(
        kept, select_ref[...], (((1,), (1,)), ((), ())), preferred_element_type=F32
    ).astype(BF16)
    part[columns * live :, :] = jnp.zeros((part.shape[0] - columns * live, LANES), BF16)
    for c in range(columns):
        part[c * live : (c + 1) * live, :] = low[:, c * LANES : (c + 1) * LANES]
    part[columns * live : (columns + 1) * live, : select.shape[1]] = select

    pl.semaphore_wait(barrier, n - 1)

    def rows_of(c):
        return pl.ds(pl.multiple_of(c * block, 16), block)

    def remote(source, target, sent, received, there):
        return pltpu.make_async_remote_copy(
            src_ref=source, dst_ref=target, send_sem=sent, recv_sem=received,
            device_id={"chan": there}, device_id_type=MESH,
        )

    def arrived(where, semaphore):
        pltpu.make_async_copy(where, where, semaphore).wait()

    def scatter(k):
        there = lax.rem(me + k, n)
        return remote(part.at[rows_of(there)], parts.at[me], s_send.at[k], s_recv.at[me], there)

    def gather(k):
        mine = whole.at[rows_of(me)]
        return remote(mine, mine, g_send.at[k], g_recv.at[me], lax.rem(me + k, n))

    def start_scatter(k, _):
        scatter(k).start()
        return 0

    lax.fori_loop(1, n, start_scatter, 0)
    rank = live_rank(lengths, thoughts, (rows, 1), 0)
    place = (lax.broadcasted_iota(jnp.int32, (rows, live), 1) == rank).astype(F32).astype(BF16)
    alive[...] = jnp.broadcast_to((rank >= 0).astype(F32), (rows, LANES))

    def fill(t, _):
        first = state_ref[fork[t]]
        for j in range(tiles):
            begin[j, pl.ds(t, states, stride=thoughts), :] = first[:, lanes[j]]
        return 0

    lax.fori_loop(0, thoughts, fill, 0)

    scaled = jnp.exp(decay_ref[...]) * (-math.log2(math.e))
    for j in range(tiles):
        for s in range(states):
            decay[j, s * 8 : (s + 1) * 8, :] = jnp.broadcast_to(
                scaled[s : s + 1, lanes[j]], (8, LANES)
            )

    def take(k, total):
        source = lax.rem(me + n - k, n)
        arrived(parts.at[source], s_recv.at[source])
        return total + parts[source].astype(F32)

    total = lax.fori_loop(1, n, take, part[rows_of(me), :].astype(F32))
    whole[rows_of(me), :] = total.astype(BF16)

    def start_gather(k, _):
        gather(k).start()
        return 0

    lax.fori_loop(1, n, start_gather, 0)

    def open_gate(p, _):
        at = pl.ds(pl.multiple_of(p * thoughts, 8), thoughts)
        gate = jax.nn.silu(gate_ref[p].astype(F32))
        for j in range(tiles):
            opened[j, at, :] = jnp.where(alive[at, :] > 0.0, gate[:, lanes[j]], 0.0)
        return 0

    lax.fori_loop(0, positions, open_gate, 0)
    def take_sum(k, _):
        source = lax.rem(me + n - k, n)
        arrived(whole.at[rows_of(source)], g_recv.at[source])
        return 0

    lax.fori_loop(1, n, take_sum, 0)

    low = jnp.concatenate([whole[c * live : (c + 1) * live, :] for c in range(columns)], axis=1)
    low = jnp.dot(place, low, preferred_element_type=F32).astype(BF16)
    select = jnp.dot(
        place, whole[columns * live : (columns + 1) * live, :], preferred_element_type=F32
    )
    for s in range(2 * states):
        spread[s] = jnp.broadcast_to(select[:, s : s + 1], (rows, LANES))
    for j in range(tiles):
        raw = jnp.dot(low, up_ref[:, lanes[j]], preferred_element_type=F32)
        raw = raw + rate_bias_ref[:, lanes[j]]
        soft = jnp.maximum(raw, 0.0) + jnp.log1p(jnp.exp(-jnp.abs(raw)))
        rate[j] = soft * alive[...]

    each = thoughts // n
    groups, owners = thoughts // 8, 8 // each
    group = (me * each) // 8

    def exchange(i, q):
        now_group = lax.rem(group + groups // 2 + i, groups)
        return remote(
            sends[i].at[pl.ds(q * each, each)], got_ref.at[me], x_send.at[i * owners + q],
            x_recv.at[me], now_group * owners + q,
        )

    own_slot = lax.rem(me, owners)
    own_copy = pltpu.make_async_copy(
        sends[-(groups // 2) % groups].at[pl.ds(own_slot * each, each)], got_ref.at[me], x_own
    )

    def one_group(i):
        now_group = lax.rem(group + groups // 2 + i, groups)
        send = sends[i]
        first = pl.multiple_of(now_group * 8, 8)

        def one_block(pair, _):
            js = [pair * 2 + m for m in range(2)]
            h = tuple(
                begin[j, pl.ds(pl.multiple_of(s * thoughts + first, 8), 8), :]
                for s in range(states) for j in js
            )
            skips = [skip_ref[j] for j in js]

            def step(p, h):
                at = pl.ds(pl.multiple_of(p * thoughts + first, 8), 8)
                rates = [rate[j, at, :] for j in js]
                inflows = [driven[j, at, :] for j in js]
                pushes = [a * b for a, b in zip(rates, inflows)]
                readouts = [a * b for a, b in zip(skips, inflows)]
                later = []
                for s in range(states):
                    into, out = spread[s, at, :], spread[states + s, at, :]
                    for m in range(2):
                        factor = jnp.exp2(rates[m] * decay[js[m], s * 8 : (s + 1) * 8, :])
                        now = factor * h[2 * s + m] + pushes[m] * into
                        readouts[m] = readouts[m] + out * now
                        later.append(now)
                for m in range(2):
                    result[js[m], pl.ds(first * stretch + p, 8, stride=stretch), :] = (
                        readouts[m] * opened[js[m], at, :]
                    )
                return tuple(later)

            h = lax.fori_loop(0, positions, step, h, unroll=2)
            for s in range(states):
                for m in range(2):
                    final[js[m], pl.ds(first * states + s, 8, stride=states), :] = h[2 * s + m]
            return 0

        lax.fori_loop(0, tiles // 2, one_block, 0)

        def pack(slot, _):
            t = first + slot
            at = pl.multiple_of(t * stretch, 8)
            for j in range(tiles):
                send[slot, :, lanes[j]] = result[j, pl.ds(at, 16), :].astype(BF16)
                send[slot, :, width + j * LANES : width + (j + 1) * LANES] = final[
                    j, pl.ds(pl.multiple_of(t * states, 8), states), :
                ].astype(BF16)
            apart = tiles // folds
            for i in range(apart):
                pieces = [
                    result[a * apart + i, pl.ds(pl.multiple_of(at + 16, 8), 8), :][: positions - 16]
                    for a in range(folds)
                ]
                if folds < 4:
                    pieces.append(jnp.zeros((16 - 4 * folds, LANES), F32))
                send[slot, :, 2 * width + i * LANES : 2 * width + (i + 1) * LANES] = jnp.concatenate(
                    pieces, axis=0
                ).astype(BF16)
            return 0

        lax.fori_loop(0, 8, pack, 0)

        def dispatch(k, _):
            q = lax.rem(me + k, owners)

            @pl.when(now_group * owners + q != me)
            def _():
                exchange(i, q).start()

            return 0

        lax.fori_loop(0, owners, dispatch, 0)
        if i == -(groups // 2) % groups:
            own_copy.start()

    for i in range(groups):
        one_group(i)

    def drain_sums(k, _):
        scatter(k).wait_send()
        gather(k).wait_send()
        return 0

    def drain_exchange(k, _):
        source = lax.rem(me + k, n)
        arrived(got_ref.at[source], x_recv.at[source])
        return 0

    for i in range(groups):
        def drain_send(q, _):
            @pl.when(lax.rem(group + groups // 2 + i, groups) * owners + q != me)
            def _():
                exchange(i, q).wait_send()

            return 0

        lax.fori_loop(0, owners, drain_send, 0)

    lax.fori_loop(1, n, drain_sums, 0)
    own_copy.wait()
    lax.fori_loop(1, n, drain_exchange, 0)


def unfold_kernel(folds, got_ref, out_ref, final_ref):
    sources, each = got_ref.shape[:2]
    positions = out_ref.shape[1]
    width = out_ref.shape[2] // sources
    for c in range(sources):
        at = slice(c * width, (c + 1) * width)
        for i in range(each):
            head = got_ref[c, i, :, :width].astype(F32)
            tail = got_ref[c, i, :, 2 * width :].astype(F32)
            tail = jnp.concatenate(
                [tail[4 * a : 4 * a + positions - 16] for a in range(folds)], axis=1
            )
            out_ref[i, :, at] = jnp.concatenate([head, tail], axis=0).astype(BF16)
            final_ref[i, :, at] = got_ref[c, i, :, width : 2 * width].astype(F32)


def vmem(count):
    return [pl.BlockSpec(memory_space=pltpu.VMEM)] * count


def smem(count):
    return [pl.BlockSpec(memory_space=pltpu.SMEM)] * count


def body(
    parent_state,
    parent_conv,
    fork_map,
    judge_lengths,
    mixer_input,
    gate_input,
    conv_weight,
    conv_bias,
    rate_down,
    selection_weight,
    rate_up,
    rate_bias,
    decay_log,
    skip_gain,
):
    n = lax.axis_size("chan")
    thoughts, positions, width = mixer_input.shape
    states, rank = parent_state.shape[1], rate_up.shape[0]
    tiles, rows = width // LANES, thoughts * positions
    live = thoughts * (GEN + JUDGE // 2)
    used = (rank // LANES + 1) * live
    block = -(-used // (16 * n)) * 16
    folds = min(4, tiles)
    each = thoughts // n
    packed = 2 * width + width // folds
    dma = pltpu.SemaphoreType.DMA

    got = pl.pallas_call(
        functools.partial(mixer_kernel, n),
        out_shape=jax.ShapeDtypeStruct((n, each, 16, packed), BF16),
        in_specs=smem(2) + vmem(12),
        out_specs=pl.BlockSpec(memory_space=pl.ANY),
        scratch_shapes=[
            pltpu.VMEM((rows, width), BF16),
            pltpu.VMEM((tiles, rows, LANES), F32),
            pltpu.VMEM((n * block, LANES), BF16),
            pltpu.VMEM((n, block, LANES), BF16),
            pltpu.VMEM((n * block, LANES), BF16),
            pltpu.VMEM((rows, LANES), F32),
            pltpu.VMEM((tiles, rows, LANES), F32),
            pltpu.VMEM((tiles, states * thoughts, LANES), F32),
            pltpu.VMEM((tiles, states * 8, LANES), F32),
            pltpu.VMEM((tiles, rows, LANES), F32),
            pltpu.VMEM((2 * states, rows, LANES), F32),
            pltpu.VMEM((tiles, thoughts * 24, LANES), F32),
            pltpu.VMEM((tiles, thoughts * states, LANES), F32),
        ] + [dma((n,))] * 6 + [dma]
        + [pltpu.VMEM((8, 16, packed), BF16)] * (thoughts // 8),
        compiler_params=pltpu.CompilerParams(
            collective_id=0, has_side_effects=True, vmem_limit_bytes=VMEM_LIMIT
        ),
        name="mixer",
    )(fork_map, judge_lengths, jnp.swapaxes(mixer_input, 0, 1), jnp.swapaxes(parent_conv, 0, 1),
      conv_weight, conv_bias[None, :], rate_down, selection_weight.T,
      jnp.swapaxes(gate_input, 0, 1), parent_state, rate_up, rate_bias[None, :], decay_log,
      skip_gain.reshape(tiles, 1, LANES))

    together = n // 2
    return pl.pallas_call(
        functools.partial(unfold_kernel, folds),
        grid=(n // together,),
        out_shape=(
            jax.ShapeDtypeStruct((each, positions, n * width), BF16),
            jax.ShapeDtypeStruct((each, states, n * width), F32),
        ),
        in_specs=[pl.BlockSpec((together, each, 16, packed), lambda c: (c, 0, 0, 0))],
        out_specs=(
            pl.BlockSpec((each, positions, together * width), lambda c: (0, 0, c)),
            pl.BlockSpec((each, states, together * width), lambda c: (0, 0, c)),
        ),
        compiler_params=pltpu.CompilerParams(vmem_limit_bytes=VMEM_LIMIT),
        name="unfold",
    )(got)


def solution(mesh):
    placed = (
        P("group", None, "chan"),
        P("group", None, "chan"),
        P("group"),
        P("group"),
        P("group", None, "chan"),
        P("group", None, "chan"),
        P(None, "chan"),
        P("chan"),
        P("chan", None),
        P("chan", None),
        P(None, "chan"),
        P("chan"),
        P(None, "chan"),
        P("chan"),
    )
    return jax.shard_map(
        body,
        mesh=mesh,
        in_specs=placed,
        out_specs=(P(("group", "chan"), None, None), P(("group", "chan"), None, None)),
        check_vma=False,
    )
```
